32 devices in a mesh: mem: 2 (over x), lat: 4 (over y, core), lon: 4 (over z).
Axes of the slice: x: 2, y: 2, z: 4, core: 2. Of those that a mesh axis runs over, the one named last changes fastest.
Arguments:
- perturb: float32 [4, 1536, 2048], P('mem', 'lat', 'lon'), may hold values from -6 to 6
- loc_lat: float32 [384], replicated, may hold values from 1 to 96
- loc_lon: float32 [512], replicated, may hold values from 1 to 128
- obs_cell: int32 [4, 4, 2048], P('lat', 'lon'), may hold values from 0 to 196607
- obs_count: int32 [4, 4], P('lat', 'lon'), may hold values from 512 to 2048, as said below
- obs_innov: float32 [4, 4, 2048], P('lat', 'lon'), may hold values from -8 to 8
- obs_error: float32 [4, 4, 2048], P('lat', 'lon'), may hold values from 0.5 to 4
Outputs:
- analysis: float32 [4, 384, 512], P('mem', 'lat', 'lon')
- increment: float32 [1536, 2048], P('lat', 'lon')
The draws below stay inside these ranges and needn't reach their ends.
Inputs may be any that keep to these rules, and one draw needn't show every extreme that they name: `obs_cell`: cells may repeat within a tile. `obs_count`: in every draw at least one tile uses all 2048 slots.
All inputs are finite; a program needn't handle non-finite values.
Results may differ from the reference program's by a relative error of at most 0.0001.
Values sent between devices are 32-bit elements; how exact they have to be, the bound alone decides.
A program may use at most 64 MiB of HBM per device.

```python
import math
import jax
import jax.numpy as jnp
from jax import lax

NLAT = 1536
NLON = 2048
ITERS = 2
CLAT = 384
CLON = 512
MEMBERS = 4
NQLAT = 384
NQLON = 512
OBS_TILE = 2048
LAT_TILES = 4
LON_TILES = 4


def draw_obs_count(key, part):
    first_key, second_key = jax.random.split(jax.random.fold_in(key, 17))
    counts = jax.random.randint(first_key, (LAT_TILES, LON_TILES), OBS_TILE // 4, OBS_TILE + 1)
    chosen = jax.random.randint(second_key, (), 0, LAT_TILES * LON_TILES)
    flat_index = jnp.arange(LAT_TILES * LON_TILES, dtype=jnp.int32).reshape(LAT_TILES, LON_TILES)
    return jnp.where(flat_index == chosen, OBS_TILE, counts).astype(jnp.int32)


def touch_ends(values, rng, low, high):
    shape = values.shape
    spot = [jax.random.randint(jax.random.fold_in(rng, axis), (), 0, shape[axis]) for axis in range(len(shape))]
    values = values.at[tuple(spot)].set(low)
    longest = shape.index(max(shape))
    spot[longest] = (spot[longest] + 1) % shape[longest]
    return values.at[tuple(spot)].set(high)


def shard_levels(key, dims, cuts, low, high):
    gain = 1.0
    for axis_at, blocks in cuts:
        heights = jax.random.uniform(jax.random.fold_in(jax.random.fold_in(key, 6), axis_at), (blocks,), jnp.float32, low / len(cuts), high / len(cuts))
        gain = gain * jnp.repeat(jnp.exp(heights), dims[axis_at] // blocks).reshape((-1,) + (1,) * (len(dims) - 1 - axis_at))
    return gain


def scatter_about(rng, dims, width, most, shards=(), held_as=jnp.bfloat16):
    gain = shard_levels(rng, dims, shards, -0.22, 0.18) if shards else 1.0
    values = jax.random.normal(rng, dims, jnp.float32) * width * gain
    return jnp.minimum(jnp.maximum(values, -most), most).astype(held_as)


def setup_inputs(seed: int = 0) -> dict:
    key_of = jax.random.split(jax.random.key(seed), 8)
    perturb = scatter_about(key_of[0], (MEMBERS, NLAT, NLON), 1.0, 6.0, ((0, 2), (1, 4), (2, 4)), jnp.float32)
    loc_lat = jnp.clip(jnp.exp(jax.random.uniform(key_of[1], (NQLAT,), jnp.float32, math.log(1.0), math.log(96.0))), 1.0, 96.0)
    loc_lon = jnp.clip(jnp.exp(jax.random.uniform(key_of[2], (NQLON,), jnp.float32, math.log(1.0), math.log(128.0))), 1.0, 128.0)
    obs_cell = touch_ends(jax.random.randint(key_of[3], (LAT_TILES, LON_TILES, OBS_TILE), 0, CLAT * CLON), jax.random.fold_in(key_of[3], 1), 0, (CLAT * CLON) - 1).astype(jnp.int32)
    obs_count = draw_obs_count(jax.random.fold_in(key_of[7], 71), 0)
    obs_innov = scatter_about(key_of[5], (LAT_TILES, LON_TILES, OBS_TILE), 2.0, 8.0, ((0, 4), (1, 4)), jnp.float32)
    obs_error = jnp.clip(jnp.exp(math.log(4.0) - 2.0794415 * jax.random.uniform(key_of[6], (LAT_TILES, LON_TILES, OBS_TILE), jnp.float32) ** shard_levels(key_of[6], (LAT_TILES, LON_TILES, OBS_TILE), ((0, 4), (1, 4)), -0.2, 0.2)), 0.5, 4.0)
    return dict(perturb=perturb, loc_lat=loc_lat, loc_lon=loc_lon, obs_cell=obs_cell, obs_count=obs_count, obs_innov=obs_innov, obs_error=obs_error)


huber_width = 1.0
tiny_floor = 1e-06
highest = lax.Precision.HIGHEST

def kernel_rows(scales, first_row, row_count):
    total_rows = scales.shape[0]
    row_index = first_row + jnp.arange(row_count, dtype=jnp.int32)
    inside = (row_index >= 0) & (row_index < total_rows)
    row_scale = scales[jnp.clip(row_index, 0, total_rows - 1)]
    col_index = jnp.arange(total_rows, dtype=jnp.int32)
    offset = (row_index[:, None] - col_index[None, :]).astype(jnp.float32)
    spread = row_scale[:, None] ** 2 + scales[None, :] ** 2
    weight = jnp.where(inside, (jnp.sqrt(jnp.pi) * row_scale) ** (-0.5), jnp.zeros_like(row_scale))
    return weight[:, None] * jnp.exp(-offset * offset / spread)

def refine_axis(coarse, along):
    coarse_count = coarse.shape[along] - 2
    lower_cells = lax.slice_in_dim(coarse, 0, coarse_count, axis=along)
    middle = lax.slice_in_dim(coarse, 1, coarse_count + 1, axis=along)
    upper_cells = lax.slice_in_dim(coarse, 2, coarse_count + 2, axis=along)
    pieces = (0.375 * lower_cells + 0.625 * middle, 0.125 * lower_cells + 0.875 * middle, 0.875 * middle + 0.125 * upper_cells, 0.625 * middle + 0.375 * upper_cells)
    stacked = jnp.stack(pieces, axis=along + 1)
    new_shape = list(coarse.shape)
    new_shape[along] = 4 * coarse_count
    return stacked.reshape(new_shape)

def refine_both(coarse):
    return refine_axis(refine_axis(coarse, coarse.ndim - 2), coarse.ndim - 1)

def reference(perturb, loc_lat, loc_lon, obs_cell, obs_count, obs_innov, obs_error):
    members = perturb.shape[0]
    member_scale = 1.0 / math.sqrt(members - 1)
    lat_kernel = kernel_rows(loc_lat, 0, NQLAT)
    lon_kernel = kernel_rows(loc_lon, 0, NQLON)
    tile_lat = jnp.arange(LAT_TILES, dtype=jnp.int32)[:, None, None]
    tile_lon = jnp.arange(LON_TILES, dtype=jnp.int32)[None, :, None]
    obs_rows = (tile_lat * CLAT + obs_cell // CLON).astype(jnp.int32)
    obs_cols = (tile_lon * CLON + obs_cell % CLON).astype(jnp.int32)
    usable = (jnp.arange(OBS_TILE, dtype=jnp.int32)[None, None, :] < obs_count[:, :, None]).astype(jnp.float32)

    def refined(control):
        coarse = jnp.dot(jnp.dot(lat_kernel, control, precision=highest), lon_kernel.T, precision=highest)
        return refine_both(jnp.pad(coarse, 1))

    def field_of(controls):

        def add_member(running, member_items):
            control, member = member_items
            return (running + refined(control) * member, None)
        running, _ = lax.scan(add_member, jnp.zeros((NLAT, NLON), jnp.float32), (controls, perturb))
        return member_scale * running

    def adjoint(weights):
        spread = jnp.zeros((NLAT, NLON), jnp.float32).at[obs_rows, obs_cols].add(weights)
        _, pullback = jax.vjp(refined, jnp.zeros((NQLAT, NQLON), jnp.float32))

        def single(member):
            return pullback(member * (member_scale * spread))[0]
        return lax.map(single, perturb)
    analysis = jnp.zeros((members, NQLAT, NQLON), jnp.float32)
    observed = jnp.zeros_like(obs_innov)
    increment = jnp.zeros((NLAT, NLON), jnp.float32)
    for iteration in range(ITERS):
        residual = (observed - obs_innov) / obs_error
        weights = usable * residual / jnp.sqrt(1.0 + (residual / huber_width) ** 2) / obs_error
        gradient = analysis + adjoint(weights)
        image_field = field_of(gradient)
        image_obs = image_field[obs_rows, obs_cols]
        grad_total = jnp.sum(gradient * gradient)
        curvature = jnp.sum(usable * (image_obs / obs_error) ** 2)
        length = grad_total / (grad_total + curvature + tiny_floor)
        analysis = analysis - length * gradient
        observed = observed - length * image_obs
        increment = increment - length * image_field
    return (analysis, increment)
```

```python
import math

import jax
import jax.numpy as jnp
from jax import lax
from jax.experimental import pallas as pl
from jax.experimental.pallas import tpu as pltpu
from jax.sharding import PartitionSpec as P

ITERS = 2
huber_width = 1.0
tiny_floor = 1e-06

NN = (((1,), (0,)), ((), ()))
NT = (((1,), (1,)), ((), ()))


def round_up(count, unit):
    return -(-count // unit) * unit


def extended_index(tiles, pad, tile, first, total):
    row = lax.broadcasted_iota(jnp.int32, (tiles * pad, 1), 0)
    at = jnp.zeros_like(row)
    for later in range(1, tiles):
        at = at + (row >= later * pad).astype(jnp.int32)
    inner = row - at * pad
    which = first - at
    which = jnp.where(which < 0, which + tiles, which)
    index = which * tile - 1 + inner
    valid = (inner < tile + 2) & (index >= 0) & (index < total)
    return index, valid


def kernel_rows(scales, index, valid):
    column = lax.broadcasted_iota(jnp.int32, (index.shape[0], scales.shape[1]), 1)
    row_scale = jnp.sum(jnp.where(column == index, scales, 0.0), axis=1, keepdims=True)
    row_scale = jnp.where(valid, row_scale, 1.0)
    offset = (index - column).astype(jnp.float32)
    weight = jnp.where(valid, lax.rsqrt(math.sqrt(math.pi) * row_scale), 0.0)
    return weight * jnp.exp(-(offset * offset) / (row_scale * row_scale + scales * scales))


def select_rows(count, first, total):
    row = lax.broadcasted_iota(jnp.int32, (count, total), 0) + first
    column = lax.broadcasted_iota(jnp.int32, (count, total), 1)
    return (row == column).astype(jnp.float32)


def interpolation(fine, pad):
    below = fine >> 2
    phase = (fine & 3).astype(jnp.float32)
    lower = jnp.maximum(0.375 - 0.25 * phase, 0.0)
    upper = jnp.maximum(0.25 * phase - 0.375, 0.0)
    middle = 1.0 - lower - upper
    cell = lax.broadcasted_iota(jnp.int32, (pad, fine.shape[1]), 0) - below
    return jnp.where(
        cell == 0,
        lower,
        jnp.where(cell == 1, middle, jnp.where(cell == 2, upper, 0.0)),
    )


def split_cell(cell, width):
    if width & (width - 1) == 0:
        row = cell >> (width.bit_length() - 1)
    else:
        row = lax.div(cell, jnp.int32(width))
    return row, cell - row * width


def split(values):
    high = values.astype(jnp.bfloat16)
    return high, (values - high.astype(jnp.float32)).astype(jnp.bfloat16)


def multiply(left, right, dims):
    return lax.dot_general(left, right, dims, preferred_element_type=jnp.float32)


def product(left, right, dims):
    if not isinstance(left, tuple):
        return multiply(left, right[0], dims) + multiply(left, right[1], dims)
    if not isinstance(right, tuple):
        return multiply(left[0], right, dims) + multiply(left[1], right, dims)
    return (
        multiply(left[0], right[0], dims)
        + multiply(left[0], right[1], dims)
        + multiply(left[1], right[0], dims)
    )


def put(ref, values):
    high, low = split(values)
    ref[0] = high
    ref[1] = low


class Plan:
    def __init__(self, perturb, slots, total_lat, total_lon, axes):
        self.members, self.fine_lat, self.fine_lon = perturb
        self.tile_lat, self.tile_lon = self.fine_lat // 4, self.fine_lon // 4
        self.slots, self.total_lat, self.total_lon = slots, total_lat, total_lon
        self.mems, self.lats, self.lons = axes
        self.pad_lat = round_up(self.tile_lat + 2, 128)
        self.pad_lon = round_up(self.tile_lon + 2, 16)
        self.scale = 1.0 / math.sqrt(self.members * self.mems - 1)
        self.chunk = math.gcd(slots, 512)
        self.share = self.mems * math.prod(perturb) <= 1 << 21
        group = self.lats * self.lons
        self.copies = (self.mems - 1) + ITERS * (
            self.lons - 1 + 2 * (self.lats - 1) + 2 * (self.mems - 1) + group - 1
        )


def body(
    plan,
    perturb,
    lat_scales,
    lon_scales,
    cell,
    count,
    innov,
    error,
    analysis,
    increment,
    others,
    column_weight,
    row_weight,
    at_obs,
    lon_factor,
    lat_factor,
    lat_grad,
    to_rows,
    to_columns,
    terms,
    strips,
    grads,
    coarses,
    images,
    sums,
    send_sem,
    recv_sem,
):
    p = plan
    at_mem, at_lat, at_lon = (lax.axis_index(name) for name in ("mem", "lat", "lon"))

    def peer(here, distance, size):
        return lax.rem(here + distance, size)

    group = [(a, b) for a in range(p.lats) for b in range(p.lons) if a or b]

    def in_group(a, b):
        return {"lat": peer(at_lat, a, p.lats), "lon": peer(at_lon, b, p.lons)}

    barrier = pltpu.get_barrier_semaphore()
    for a, b in group:
        pl.semaphore_signal(
            barrier, inc=1, device_id=in_group(a, b), device_id_type=pl.DeviceIdType.MESH
        )
    for d in range(1, p.mems):
        pl.semaphore_signal(
            barrier,
            inc=1,
            device_id={"mem": peer(at_mem, d, p.mems)},
            device_id_type=pl.DeviceIdType.MESH,
        )
    pl.semaphore_wait(barrier, len(group) + p.mems - 1)

    started = []

    def send(source, target, device):
        at = len(started)
        copy = pltpu.make_async_remote_copy(
            src_ref=source,
            dst_ref=target,
            send_sem=send_sem.at[at],
            recv_sem=recv_sem.at[at],
            device_id=device,
            device_id_type=pl.DeviceIdType.MESH,
        )
        copy.start()
        started.append(copy)
        return copy

    def spread_out(ref, axis, here, size):
        return [
            send(ref.at[0], ref.at[d], {axis: peer(here, d, size)}) for d in range(1, size)
        ]

    def receive(copies):
        for copy in copies:
            copy.wait_recv()

    late = []
    if p.share:
        late += [
            send(perturb, others.at[d - 1], {"mem": peer(at_mem, d, p.mems)})
            for d in range(1, p.mems)
        ]

    row, column = split_cell(cell[...], p.fine_lon)
    row_weight[...] = interpolation(row, p.pad_lat).astype(jnp.bfloat16)
    column_weight[...] = interpolation(column, p.pad_lon)
    for start in range(0, p.slots, p.chunk):
        here = slice(start, start + p.chunk)
        chosen = lax.broadcasted_iota(jnp.int32, (p.fine_lon, p.chunk), 0) == column[:, here]
        chosen = chosen.astype(jnp.float32).astype(jnp.bfloat16)
        wanted = lax.broadcasted_iota(jnp.int32, (p.fine_lat, p.chunk), 0) == row[:, here]
        for k in range(p.members):
            picked = product(split(perturb[k]), chosen, NN)
            at_obs[k : k + 1, here] = p.scale * jnp.sum(
                jnp.where(wanted, picked, 0.0), axis=0, keepdims=True
            )

    lon_ext = kernel_rows(
        lon_scales[...], *extended_index(p.lons, p.pad_lon, p.tile_lon, at_lon, p.total_lon)
    )
    lon_ext = split(lon_ext)
    own_rows = p.pad_lon
    lon_own = tuple(term[:own_rows] for term in lon_ext)
    put(lon_factor.at[:, :own_rows], product(lon_own, lon_ext, NT))
    picks = select_rows(p.tile_lon, at_lon * p.tile_lon, p.total_lon).astype(jnp.bfloat16)
    put(lon_factor.at[:, own_rows:], product(picks, lon_ext, NT))
    lat_ext = kernel_rows(
        lat_scales[...], *extended_index(p.lats, p.pad_lat, p.tile_lat, at_lat, p.total_lat)
    )
    lat_ext = split(lat_ext)
    lat_own = tuple(term[: p.pad_lat] for term in lat_ext)
    put(lat_factor, product(lat_ext, lat_own, NT))
    picks = select_rows(p.tile_lat, at_lat * p.tile_lat, p.total_lat).astype(jnp.bfloat16)
    put(lat_grad, product(picks, lat_ext, NT))
    to_rows[...] = interpolation(
        lax.broadcasted_iota(jnp.int32, (1, p.fine_lat), 1), p.pad_lat
    ).astype(jnp.bfloat16)
    to_columns[...] = interpolation(
        lax.broadcasted_iota(jnp.int32, (1, p.fine_lon), 1), p.pad_lon
    ).astype(jnp.bfloat16)

    usable = lax.broadcasted_iota(jnp.int32, (1, p.slots), 1) < count[...]
    usable = usable.astype(jnp.float32)
    inverse = 1.0 / error[...]
    observed = jnp.zeros((1, p.slots), jnp.float32)
    dual = jnp.zeros((1, p.slots), jnp.float32)
    lengths, grad_copies, coarse_copies = [], [], []
    for it in range(ITERS):
        residual = (observed - innov[...]) * inverse
        bounded = residual * lax.rsqrt(1.0 + (residual / huber_width) ** 2)
        step = dual + usable * bounded * inverse
        term, strip, grad = terms.at[it], strips.at[it], grads.at[it]
        for k in range(p.members):
            weighted = split(column_weight[...] * (step * at_obs[k : k + 1, :]))
            term[0, k * p.pad_lon : (k + 1) * p.pad_lon] = product(weighted, row_weight[...], NT)
        receive(spread_out(term, "lon", at_lon, p.lons))
        pieces = [
            (
                split(
                    jnp.concatenate(
                        [
                            term[d, k * p.pad_lon : (k + 1) * p.pad_lon]
                            for d in range(p.lons)
                        ]
                    )
                )
            )
            for k in range(p.members)
        ]
        for k in range(p.members):
            near = (lon_factor[0, :own_rows], lon_factor[1, :own_rows])
            strip[0, k * p.pad_lon : (k + 1) * p.pad_lon] = product(near, pieces[k], NN)
        strip_copies = spread_out(strip, "lat", at_lat, p.lats)
        for k in range(p.members):
            near = (lon_factor[0, own_rows:], lon_factor[1, own_rows:])
            grad[0, k * p.tile_lon : (k + 1) * p.tile_lon] = product(near, pieces[k], NN)
        receive(strip_copies)
        coarse = None
        for d in range(p.lats):
            there = slice(d * p.pad_lat, (d + 1) * p.pad_lat)
            part = product(split(strip[d]), (lat_factor[0, there], lat_factor[1, there]), NN)
            coarse = part if coarse is None else coarse + part
        coarses[it, 0] = coarse
        image = jnp.zeros((1, p.slots), jnp.float32)
        for k in range(p.members):
            rows = product(
                split(coarse[k * p.pad_lon : (k + 1) * p.pad_lon]), row_weight[...], NN
            )
            image = image + at_obs[k : k + 1, :] * jnp.sum(
                rows * column_weight[...], axis=0, keepdims=True
            )
        images[it, 0] = image
        image_copies = spread_out(images.at[it], "mem", at_mem, p.mems)
        if p.share:
            late += spread_out(coarses.at[it], "mem", at_mem, p.mems)
        late += spread_out(grad, "lat", at_lat, p.lats)
        receive(image_copies)
        for d in range(1, p.mems):
            image = image + images[it, d]
        grad_part = jnp.sum(step * image, axis=1, keepdims=True)
        curve_part = jnp.sum(usable * (image * inverse) ** 2, axis=1, keepdims=True)
        first = lax.broadcasted_iota(jnp.int32, (8, 128), 0) == 0
        sums[it, 0] = jnp.where(first, grad_part, curve_part)
        receive(
            [
                send(sums.at[it, 0], sums.at[it, a * p.lons + b], in_group(a, b))
                for a, b in group
            ]
        )
        total = jnp.sum(sums[it], axis=0)
        grad_total, curvature = total[0:1, 0:1], total[1:2, 0:1]
        length = grad_total / (grad_total + curvature + tiny_floor)
        lengths.append(length)
        observed = observed - length * image
        dual = dual - length * step
    receive(late)

    def combined(ref, place):
        return -sum(lengths[it] * ref[(it,) + place] for it in range(ITERS))

    for k in range(p.members):
        own = None
        for d in range(p.lats):
            there = slice(d * p.pad_lat, (d + 1) * p.pad_lat)
            strip = split(combined(grads, (d, slice(k * p.tile_lon, (k + 1) * p.tile_lon))))
            part = product((lat_grad[0, :, there], lat_grad[1, :, there]), strip, NT)
            own = part if own is None else own + part
        analysis[k] = own
    field = None
    for d in range(p.mems if p.share else 1):
        partial = None
        for k in range(p.members):
            coarse = combined(coarses, (d, slice(k * p.pad_lon, (k + 1) * p.pad_lon)))
            wide = lax.dot_general(
                to_rows[...],
                split(coarse)[0],
                (((0,), (1,)), ((), ())),
                preferred_element_type=jnp.float32,
            ) + lax.dot_general(
                to_rows[...],
                split(coarse)[1],
                (((0,), (1,)), ((), ())),
                preferred_element_type=jnp.float32,
            )
            fine = product(split(wide), to_columns[...], NN)
            here = perturb[k] if d == 0 else others[d - 1, k]
            partial = fine * here if partial is None else partial + fine * here
        field = partial if field is None else field + partial
    increment[...] = p.scale * field
    for copy in started:
        copy.wait_send()


def per_device(perturb, loc_lat, loc_lon, obs_cell, obs_count, obs_innov, obs_error):
    p = Plan(
        perturb.shape,
        obs_cell.shape[-1],
        loc_lat.shape[0],
        loc_lon.shape[0],
        tuple(lax.axis_size(name) for name in ("mem", "lat", "lon")),
    )
    f32, bf16 = jnp.float32, jnp.bfloat16
    coarse_rows = p.members * p.pad_lon
    grad_rows = p.members * p.tile_lon
    in_vmem = pl.BlockSpec(memory_space=pltpu.VMEM)
    groups = p.mems if p.share else 1
    analysis, increment = pl.pallas_call(
        lambda *refs: body(p, *refs),
        out_shape=(
            jax.ShapeDtypeStruct((p.members, p.tile_lat, p.tile_lon), f32),
            jax.ShapeDtypeStruct((p.fine_lat, p.fine_lon), f32),
        ),
        in_specs=[in_vmem] * 7,
        out_specs=(in_vmem, in_vmem),
        scratch_shapes=[
            pltpu.VMEM((max(groups - 1, 1),) + perturb.shape, f32),
            pltpu.VMEM((p.pad_lon, p.slots), f32),
            pltpu.VMEM((p.pad_lat, p.slots), bf16),
            pltpu.VMEM((p.members, p.slots), f32),
            pltpu.VMEM((2, p.pad_lon + p.tile_lon, p.lons * p.pad_lon), bf16),
            pltpu.VMEM((2, p.lats * p.pad_lat, p.pad_lat), bf16),
            pltpu.VMEM((2, p.tile_lat, p.lats * p.pad_lat), bf16),
            pltpu.VMEM((p.pad_lat, p.fine_lat), bf16),
            pltpu.VMEM((p.pad_lon, p.fine_lon), bf16),
            pltpu.VMEM((ITERS, p.lons, coarse_rows, p.pad_lat), f32),
            pltpu.VMEM((ITERS, p.lats, coarse_rows, p.pad_lat), f32),
            pltpu.VMEM((ITERS, p.lats, grad_rows, p.pad_lat), f32),
            pltpu.VMEM((ITERS, groups, coarse_rows, p.pad_lat), f32),
            pltpu.VMEM((ITERS, p.mems, 1, p.slots), f32),
            pltpu.VMEM((ITERS, p.lats * p.lons, 8, 128), f32),
            pltpu.SemaphoreType.DMA((p.copies,)),
            pltpu.SemaphoreType.DMA((p.copies,)),
        ],
        compiler_params=pltpu.CompilerParams(
            collective_id=0, has_side_effects=True, vmem_limit_bytes=48 << 20
        ),
    )(
        perturb,
        loc_lat.reshape(1, -1),
        loc_lon.reshape(1, -1),
        obs_cell.reshape(1, -1),
        obs_count,
        obs_innov.reshape(1, -1),
        obs_error.reshape(1, -1),
    )
    if not p.share:
        increment = lax.psum(increment, "mem")
    return analysis, increment


def solution(mesh):
    placed = (
        P("mem", "lat", "lon"),
        P(),
        P(),
        P("lat", "lon", None),
        P("lat", "lon"),
        P("lat", "lon", None),
        P("lat", "lon", None),
    )
    return jax.shard_map(
        per_device,
        mesh=mesh,
        in_specs=placed,
        out_specs=(P("mem", "lat", "lon"), P("lat", "lon")),
        check_vma=False,
    )
```

```python
import math

import jax
import jax.numpy as jnp
from jax import lax
from jax.experimental import pallas as pl
from jax.experimental.pallas import tpu as pltpu
from jax.sharding import PartitionSpec as P

ITERS = 2
huber_width = 1.0
tiny_floor = 1e-06

NN = (((1,), (0,)), ((), ()))
NT = (((1,), (1,)), ((), ()))


def round_up(count, unit):
    return -(-count // unit) * unit


def extended_index(tiles, pad, tile, first, total):
    row = lax.broadcasted_iota(jnp.int32, (tiles * pad, 1), 0)
    at = jnp.zeros_like(row)
    for later in range(1, tiles):
        at = at + (row >= later * pad).astype(jnp.int32)
    inner = row - at * pad
    which = first - at
    which = jnp.where(which < 0, which + tiles, which)
    index = which * tile - 1 + inner
    valid = (inner < tile + 2) & (index >= 0) & (index < total)
    return index, valid


def kernel_rows(scales, index, valid):
    column = lax.broadcasted_iota(jnp.int32, (index.shape[0], scales.shape[1]), 1)
    row_scale = jnp.sum(jnp.where(column == index, scales, 0.0), axis=1, keepdims=True)
    row_scale = jnp.where(valid, row_scale, 1.0)
    offset = (index - column).astype(jnp.float32)
    weight = jnp.where(valid, lax.rsqrt(math.sqrt(math.pi) * row_scale), 0.0)
    return weight * jnp.exp(-(offset * offset) / (row_scale * row_scale + scales * scales))


def select_rows(count, first, total):
    row = lax.broadcasted_iota(jnp.int32, (count, total), 0) + first
    column = lax.broadcasted_iota(jnp.int32, (count, total), 1)
    return (row == column).astype(jnp.float32)


def interpolation(fine, pad):
    below = fine >> 2
    phase = (fine & 3).astype(jnp.float32)
    lower = jnp.maximum(0.375 - 0.25 * phase, 0.0)
    upper = jnp.maximum(0.25 * phase - 0.375, 0.0)
    middle = 1.0 - lower - upper
    cell = lax.broadcasted_iota(jnp.int32, (pad, fine.shape[1]), 0) - below
    return jnp.where(
        cell == 0,
        lower,
        jnp.where(cell == 1, middle, jnp.where(cell == 2, upper, 0.0)),
    )


def split_cell(cell, width):
    if width & (width - 1) == 0:
        row = cell >> (width.bit_length() - 1)
    else:
        row = lax.div(cell, jnp.int32(width))
    return row, cell - row * width


def split(values):
    high = values.astype(jnp.bfloat16)
    return high, (values - high.astype(jnp.float32)).astype(jnp.bfloat16)


def multiply(left, right, dims):
    return lax.dot_general(left, right, dims, preferred_element_type=jnp.float32)


def product(left, right, dims):
    if not isinstance(left, tuple):
        return multiply(left, right[0], dims) + multiply(left, right[1], dims)
    if not isinstance(right, tuple):
        return multiply(left[0], right, dims) + multiply(left[1], right, dims)
    return (
        multiply(left[0], right[0], dims)
        + multiply(left[0], right[1], dims)
        + multiply(left[1], right[0], dims)
    )


def put(ref, values):
    high, low = split(values)
    ref[0] = high
    ref[1] = low


class Plan:
    def __init__(self, perturb, slots, total_lat, total_lon, axes):
        self.members, self.fine_lat, self.fine_lon = perturb
        self.tile_lat, self.tile_lon = self.fine_lat // 4, self.fine_lon // 4
        self.slots, self.total_lat, self.total_lon = slots, total_lat, total_lon
        self.mems, self.lats, self.lons = axes
        self.pad_lat = round_up(self.tile_lat + 2, 128)
        self.pad_lon = round_up(self.tile_lon + 2, 16)
        self.scale = 1.0 / math.sqrt(self.members * self.mems - 1)
        self.chunk = math.gcd(slots, 512)
        self.share = self.mems * math.prod(perturb) <= 1 << 21
        group = self.lats * self.lons
        self.copies = (self.mems - 1) + ITERS * (
            self.members * (self.lons - 1)
            + self.members * (self.lats - 1)
            + self.lats - 1
            + 2 * (self.mems - 1)
            + group - 1
        )


def body(
    plan,
    perturb_in,
    lat_scales_in,
    lon_scales_in,
    cell_in,
    count_in,
    innov_in,
    error_in,
    analysis,
    increment,
    perturb,
    lat_scales,
    lon_scales,
    cell,
    count,
    innov,
    error,
    load_sem,
    others,
    column_weight,
    row_weight,
    at_obs,
    lon_factor,
    lat_factor,
    lat_grad,
    to_rows,
    to_columns,
    terms,
    strips,
    grads,
    coarses,
    images,
    sums,
    send_sem,
    recv_sem,
):
    p = plan
    loads = []
    for at, (source, target) in enumerate(
        [
            (cell_in, cell),
            (perturb_in, perturb),
            (count_in, count),
            (innov_in, innov),
            (error_in, error),
            (lon_scales_in, lon_scales),
            (lat_scales_in, lat_scales),
        ]
    ):
        loads.append(pltpu.make_async_copy(source, target, load_sem.at[at]))
        loads[-1].start()
    at_mem, at_lat, at_lon = (lax.axis_index(name) for name in ("mem", "lat", "lon"))

    def peer(here, distance, size):
        return lax.rem(here + distance, size)

    group = [(a, b) for a in range(p.lats) for b in range(p.lons) if a or b]

    def in_group(a, b):
        return {"lat": peer(at_lat, a, p.lats), "lon": peer(at_lon, b, p.lons)}

    barrier = pltpu.get_barrier_semaphore()
    for a, b in group:
        pl.semaphore_signal(
            barrier, inc=1, device_id=in_group(a, b), device_id_type=pl.DeviceIdType.MESH
        )
    for d in range(1, p.mems):
        pl.semaphore_signal(
            barrier,
            inc=1,
            device_id={"mem": peer(at_mem, d, p.mems)},
            device_id_type=pl.DeviceIdType.MESH,
        )
    pl.semaphore_wait(barrier, len(group) + p.mems - 1)

    started = []

    def send(source, target, device):
        at = len(started)
        copy = pltpu.make_async_remote_copy(
            src_ref=source,
            dst_ref=target,
            send_sem=send_sem.at[at],
            recv_sem=recv_sem.at[at],
            device_id=device,
            device_id_type=pl.DeviceIdType.MESH,
        )
        copy.start()
        started.append(copy)
        return copy

    def spread_out(ref, axis, here, size, rows=slice(None)):
        return [
            send(ref.at[0, rows], ref.at[d, rows], {axis: peer(here, d, size)})
            for d in range(1, size)
        ]

    def receive(copies):
        for copy in copies:
            copy.wait_recv()

    late = []
    if p.share:
        late += [
            send(perturb_in, others.at[d - 1], {"mem": peer(at_mem, d, p.mems)})
            for d in range(1, p.mems)
        ]

    loads[0].wait()
    row, column = split_cell(cell[...], p.fine_lon)
    row_weight[...] = interpolation(row, p.pad_lat).astype(jnp.bfloat16)
    column_weight[...] = interpolation(column, p.pad_lon)
    loads[1].wait()
    for start in range(0, p.slots, p.chunk):
        here = slice(start, start + p.chunk)
        chosen = lax.broadcasted_iota(jnp.int32, (p.fine_lon, p.chunk), 0) == column[:, here]
        chosen = chosen.astype(jnp.float32).astype(jnp.bfloat16)
        wanted = lax.broadcasted_iota(jnp.int32, (p.fine_lat, p.chunk), 0) == row[:, here]
        for k in range(p.members):
            picked = product(split(perturb[k]), chosen, NN)
            at_obs[k : k + 1, here] = p.scale * jnp.sum(
                jnp.where(wanted, picked, 0.0), axis=0, keepdims=True
            )

    own_rows = p.pad_lon

    def form_lon_factors():
        lon_ext = kernel_rows(
            lon_scales[...], *extended_index(p.lons, p.pad_lon, p.tile_lon, at_lon, p.total_lon)
        )
        lon_ext = split(lon_ext)
        lon_own = tuple(term[:own_rows] for term in lon_ext)
        put(lon_factor.at[:, :own_rows], product(lon_own, lon_ext, NT))
        picks = select_rows(p.tile_lon, at_lon * p.tile_lon, p.total_lon).astype(jnp.bfloat16)
        put(lon_factor.at[:, own_rows:], product(picks, lon_ext, NT))

    def form_lat_factors():
        lat_ext = kernel_rows(
            lat_scales[...], *extended_index(p.lats, p.pad_lat, p.tile_lat, at_lat, p.total_lat)
        )
        lat_ext = split(lat_ext)
        lat_own = tuple(term[: p.pad_lat] for term in lat_ext)
        put(lat_factor, product(lat_ext, lat_own, NT))
        picks = select_rows(p.tile_lat, at_lat * p.tile_lat, p.total_lat).astype(jnp.bfloat16)
        put(lat_grad, product(picks, lat_ext, NT))
        to_rows[...] = interpolation(
            lax.broadcasted_iota(jnp.int32, (1, p.fine_lat), 1), p.pad_lat
        ).astype(jnp.bfloat16)
        to_columns[...] = interpolation(
            lax.broadcasted_iota(jnp.int32, (1, p.fine_lon), 1), p.pad_lon
        ).astype(jnp.bfloat16)

    for load in loads[2:]:
        load.wait()
    usable = lax.broadcasted_iota(jnp.int32, (1, p.slots), 1) < count[...]
    usable = usable.astype(jnp.float32)
    inverse = 1.0 / error[...]
    observed = jnp.zeros((1, p.slots), jnp.float32)
    dual = jnp.zeros((1, p.slots), jnp.float32)
    lengths, grad_copies, coarse_copies = [], [], []
    for it in range(ITERS):
        residual = (observed - innov[...]) * inverse
        bounded = residual * lax.rsqrt(1.0 + (residual / huber_width) ** 2)
        step = dual + usable * bounded * inverse
        term, strip, grad = terms.at[it], strips.at[it], grads.at[it]
        spans = [slice(k * p.pad_lon, (k + 1) * p.pad_lon) for k in range(p.members)]
        term_copies, strip_copies, pieces = [], [], []
        for k in range(p.members):
            weighted = split(column_weight[...] * (step * at_obs[k : k + 1, :]))
            term[0, spans[k]] = product(weighted, row_weight[...], NT)
            term_copies.append(spread_out(term, "lon", at_lon, p.lons, spans[k]))
        if it == 0:
            form_lon_factors()
        for k in range(p.members):
            receive(term_copies[k])
            pieces.append(split(jnp.concatenate([term[d, spans[k]] for d in range(p.lons)])))
            near = (lon_factor[0, :own_rows], lon_factor[1, :own_rows])
            strip[0, spans[k]] = product(near, pieces[k], NN)
            strip_copies.append(spread_out(strip, "lat", at_lat, p.lats, spans[k]))
        for k in range(p.members):
            near = (lon_factor[0, own_rows:], lon_factor[1, own_rows:])
            grad[0, k * p.tile_lon : (k + 1) * p.tile_lon] = product(near, pieces[k], NN)
        if it == 0:
            form_lat_factors()
        image = jnp.zeros((1, p.slots), jnp.float32)
        for k in range(p.members):
            receive(strip_copies[k])
            coarse = None
            for d in range(p.lats):
                there = slice(d * p.pad_lat, (d + 1) * p.pad_lat)
                near = (lat_factor[0, there], lat_factor[1, there])
                part = product(split(strip[d, spans[k]]), near, NN)
                coarse = part if coarse is None else coarse + part
            coarses[it, 0, spans[k]] = coarse
            rows = product(split(coarse), row_weight[...], NN)
            image = image + at_obs[k : k + 1, :] * jnp.sum(
                rows * column_weight[...], axis=0, keepdims=True
            )
        images[it, 0] = image
        image_copies = spread_out(images.at[it], "mem", at_mem, p.mems)
        if p.share:
            late += spread_out(coarses.at[it], "mem", at_mem, p.mems)
        late += spread_out(grad, "lat", at_lat, p.lats)
        receive(image_copies)
        for d in range(1, p.mems):
            image = image + images[it, d]
        grad_part = jnp.sum(step * image, axis=1, keepdims=True)
        curve_part = jnp.sum(usable * (image * inverse) ** 2, axis=1, keepdims=True)
        first = lax.broadcasted_iota(jnp.int32, (8, 128), 0) == 0
        sums[it, 0] = jnp.where(first, grad_part, curve_part)
        receive(
            [
                send(sums.at[it, 0], sums.at[it, a * p.lons + b], in_group(a, b))
                for a, b in group
            ]
        )
        total = jnp.sum(sums[it], axis=0)
        grad_total, curvature = total[0:1, 0:1], total[1:2, 0:1]
        length = grad_total / (grad_total + curvature + tiny_floor)
        lengths.append(length)
        observed = observed - length * image
        dual = dual - length * step
    receive(late)

    def combined(ref, place):
        return -sum(lengths[it] * ref[(it,) + place] for it in range(ITERS))

    for k in range(p.members):
        own = None
        for d in range(p.lats):
            there = slice(d * p.pad_lat, (d + 1) * p.pad_lat)
            strip = split(combined(grads, (d, slice(k * p.tile_lon, (k + 1) * p.tile_lon))))
            part = product((lat_grad[0, :, there], lat_grad[1, :, there]), strip, NT)
            own = part if own is None else own + part
        analysis[k] = own
    field = None
    for d in range(p.mems if p.share else 1):
        partial = None
        for k in range(p.members):
            coarse = combined(coarses, (d, slice(k * p.pad_lon, (k + 1) * p.pad_lon)))
            wide = lax.dot_general(
                to_rows[...],
                split(coarse)[0],
                (((0,), (1,)), ((), ())),
                preferred_element_type=jnp.float32,
            ) + lax.dot_general(
                to_rows[...],
                split(coarse)[1],
                (((0,), (1,)), ((), ())),
                preferred_element_type=jnp.float32,
            )
            fine = product(split(wide), to_columns[...], NN)
            here = perturb[k] if d == 0 else others[d - 1, k]
            partial = fine * here if partial is None else partial + fine * here
        field = partial if field is None else field + partial
    increment[...] = p.scale * field
    for copy in started:
        copy.wait_send()


def per_device(perturb, loc_lat, loc_lon, obs_cell, obs_count, obs_innov, obs_error):
    p = Plan(
        perturb.shape,
        obs_cell.shape[-1],
        loc_lat.shape[0],
        loc_lon.shape[0],
        tuple(lax.axis_size(name) for name in ("mem", "lat", "lon")),
    )
    f32, bf16 = jnp.float32, jnp.bfloat16
    coarse_rows = p.members * p.pad_lon
    grad_rows = p.members * p.tile_lon
    in_vmem = pl.BlockSpec(memory_space=pltpu.VMEM)
    groups = p.mems if p.share else 1
    analysis, increment = pl.pallas_call(
        lambda *refs: body(p, *refs),
        out_shape=(
            jax.ShapeDtypeStruct((p.members, p.tile_lat, p.tile_lon), f32),
            jax.ShapeDtypeStruct((p.fine_lat, p.fine_lon), f32),
        ),
        in_specs=[pl.BlockSpec(memory_space=pl.ANY)] * 7,
        out_specs=(in_vmem, in_vmem),
        scratch_shapes=[
            pltpu.VMEM(perturb.shape, f32),
            pltpu.VMEM((1, p.total_lat), f32),
            pltpu.VMEM((1, p.total_lon), f32),
            pltpu.VMEM((1, p.slots), jnp.int32),
            pltpu.VMEM((1, 1), jnp.int32),
            pltpu.VMEM((1, p.slots), f32),
            pltpu.VMEM((1, p.slots), f32),
            pltpu.SemaphoreType.DMA((7,)),
            pltpu.VMEM((max(groups - 1, 1),) + perturb.shape, f32),
            pltpu.VMEM((p.pad_lon, p.slots), f32),
            pltpu.VMEM((p.pad_lat, p.slots), bf16),
            pltpu.VMEM((p.members, p.slots), f32),
            pltpu.VMEM((2, p.pad_lon + p.tile_lon, p.lons * p.pad_lon), bf16),
            pltpu.VMEM((2, p.lats * p.pad_lat, p.pad_lat), bf16),
            pltpu.VMEM((2, p.tile_lat, p.lats * p.pad_lat), bf16),
            pltpu.VMEM((p.pad_lat, p.fine_lat), bf16),
            pltpu.VMEM((p.pad_lon, p.fine_lon), bf16),
            pltpu.VMEM((ITERS, p.lons, coarse_rows, p.pad_lat), f32),
            pltpu.VMEM((ITERS, p.lats, coarse_rows, p.pad_lat), f32),
            pltpu.VMEM((ITERS, p.lats, grad_rows, p.pad_lat), f32),
            pltpu.VMEM((ITERS, groups, coarse_rows, p.pad_lat), f32),
            pltpu.VMEM((ITERS, p.mems, 1, p.slots), f32),
            pltpu.VMEM((ITERS, p.lats * p.lons, 8, 128), f32),
            pltpu.SemaphoreType.DMA((p.copies,)),
            pltpu.SemaphoreType.DMA((p.copies,)),
        ],
        compiler_params=pltpu.CompilerParams(
            collective_id=0, has_side_effects=True, vmem_limit_bytes=48 << 20
        ),
    )(
        perturb,
        loc_lat.reshape(1, -1),
        loc_lon.reshape(1, -1),
        obs_cell.reshape(1, -1),
        obs_count,
        obs_innov.reshape(1, -1),
        obs_error.reshape(1, -1),
    )
    if not p.share:
        increment = lax.psum(increment, "mem")
    return analysis, increment


def solution(mesh):
    placed = (
        P("mem", "lat", "lon"),
        P(),
        P(),
        P("lat", "lon", None),
        P("lat", "lon"),
        P("lat", "lon", None),
        P("lat", "lon", None),
    )
    return jax.shard_map(
        per_device,
        mesh=mesh,
        in_specs=placed,
        out_specs=(P("mem", "lat", "lon"), P("lat", "lon")),
        check_vma=False,
    )
```

```python
import math

import jax
import jax.numpy as jnp
from jax import lax
from jax.experimental import pallas as pl
from jax.experimental.pallas import tpu as pltpu
from jax.sharding import PartitionSpec as P

ITERS = 2
huber_width = 1.0
tiny_floor = 1e-06

NN = (((1,), (0,)), ((), ()))
NT = (((1,), (1,)), ((), ()))


def round_up(count, unit):
    return -(-count // unit) * unit


def extended_index(tiles, pad, tile, first, total):
    row = lax.broadcasted_iota(jnp.int32, (tiles * pad, 1), 0)
    at = jnp.zeros_like(row)
    for later in range(1, tiles):
        at = at + (row >= later * pad).astype(jnp.int32)
    inner = row - at * pad
    which = first - at
    which = jnp.where(which < 0, which + tiles, which)
    index = which * tile - 1 + inner
    valid = (inner < tile + 2) & (index >= 0) & (index < total)
    return index, valid


def kernel_rows(scales, index, valid):
    column = lax.broadcasted_iota(jnp.int32, (index.shape[0], scales.shape[1]), 1)
    row_scale = jnp.sum(jnp.where(column == index, scales, 0.0), axis=1, keepdims=True)
    row_scale = jnp.where(valid, row_scale, 1.0)
    offset = (index - column).astype(jnp.float32)
    weight = jnp.where(valid, lax.rsqrt(math.sqrt(math.pi) * row_scale), 0.0)
    return weight * jnp.exp(-(offset * offset) / (row_scale * row_scale + scales * scales))


def select_rows(count, first, total):
    row = lax.broadcasted_iota(jnp.int32, (count, total), 0) + first
    column = lax.broadcasted_iota(jnp.int32, (count, total), 1)
    return (row == column).astype(jnp.float32)


def interpolation(fine, pad):
    below = fine >> 2
    phase = (fine & 3).astype(jnp.float32)
    lower = jnp.maximum(0.375 - 0.25 * phase, 0.0)
    upper = jnp.maximum(0.25 * phase - 0.375, 0.0)
    middle = 1.0 - lower - upper
    cell = lax.broadcasted_iota(jnp.int32, (pad, fine.shape[1]), 0) - below
    return jnp.where(
        cell == 0,
        lower,
        jnp.where(cell == 1, middle, jnp.where(cell == 2, upper, 0.0)),
    )


def split_cell(cell, width):
    if width & (width - 1) == 0:
        row = cell >> (width.bit_length() - 1)
    else:
        row = lax.div(cell, jnp.int32(width))
    return row, cell - row * width


def split(values):
    high = values.astype(jnp.bfloat16)
    return high, (values - high.astype(jnp.float32)).astype(jnp.bfloat16)


def multiply(left, right, dims):
    return lax.dot_general(left, right, dims, preferred_element_type=jnp.float32)


def product(left, right, dims):
    if not isinstance(left, tuple):
        return multiply(left, right[0], dims) + multiply(left, right[1], dims)
    if not isinstance(right, tuple):
        return multiply(left[0], right, dims) + multiply(left[1], right, dims)
    return (
        multiply(left[0], right[0], dims)
        + multiply(left[0], right[1], dims)
        + multiply(left[1], right[0], dims)
    )


def put(ref, values):
    high, low = split(values)
    ref[0] = high
    ref[1] = low


class Plan:
    def __init__(self, perturb, slots, total_lat, total_lon, axes):
        self.members, self.fine_lat, self.fine_lon = perturb
        self.tile_lat, self.tile_lon = self.fine_lat // 4, self.fine_lon // 4
        self.slots, self.total_lat, self.total_lon = slots, total_lat, total_lon
        self.mems, self.lats, self.lons = axes
        self.pad_lat = round_up(self.tile_lat + 2, 128)
        self.pad_lon = round_up(self.tile_lon + 2, 16)
        self.scale = 1.0 / math.sqrt(self.members * self.mems - 1)
        self.chunk = math.gcd(slots, 512)
        self.share = self.mems * math.prod(perturb) <= 1 << 21
        group = self.lats * self.lons
        self.copies = ITERS * (self.mems - 1) + ITERS * (
            self.members * (self.lons - 1)
            + self.members * (self.lats - 1)
            + self.lats - 1
            + 2 * (self.mems - 1)
            + group - 1
        )


def body(
    plan,
    perturb_in,
    lat_scales_in,
    lon_scales_in,
    cell_in,
    count_in,
    innov_in,
    error_in,
    analysis,
    increment,
    perturb,
    lat_scales,
    lon_scales,
    cell,
    count,
    innov,
    error,
    load_sem,
    others,
    column_weight,
    row_weight,
    at_obs,
    lon_factor,
    lat_factor,
    lat_grad,
    to_rows,
    to_columns,
    terms,
    strips,
    grads,
    coarses,
    images,
    sums,
    send_sem,
    recv_sem,
):
    p = plan
    loads = []
    for at, (source, target) in enumerate(
        [
            (cell_in, cell),
            (perturb_in, perturb),
            (count_in, count),
            (innov_in, innov),
            (error_in, error),
            (lon_scales_in, lon_scales),
            (lat_scales_in, lat_scales),
        ]
    ):
        loads.append(pltpu.make_async_copy(source, target, load_sem.at[at]))
        loads[-1].start()
    at_mem, at_lat, at_lon = (lax.axis_index(name) for name in ("mem", "lat", "lon"))

    def peer(here, distance, size):
        return lax.rem(here + distance, size)

    group = [(a, b) for a in range(p.lats) for b in range(p.lons) if a or b]

    def in_group(a, b):
        return {"lat": peer(at_lat, a, p.lats), "lon": peer(at_lon, b, p.lons)}

    barrier = pltpu.get_barrier_semaphore()
    for a, b in group:
        pl.semaphore_signal(
            barrier, inc=1, device_id=in_group(a, b), device_id_type=pl.DeviceIdType.MESH
        )
    for d in range(1, p.mems):
        pl.semaphore_signal(
            barrier,
            inc=1,
            device_id={"mem": peer(at_mem, d, p.mems)},
            device_id_type=pl.DeviceIdType.MESH,
        )
    pl.semaphore_wait(barrier, len(group) + p.mems - 1)

    started = []

    def send(source, target, device):
        at = len(started)
        copy = pltpu.make_async_remote_copy(
            src_ref=source,
            dst_ref=target,
            send_sem=send_sem.at[at],
            recv_sem=recv_sem.at[at],
            device_id=device,
            device_id_type=pl.DeviceIdType.MESH,
        )
        copy.start()
        started.append(copy)
        return copy

    def spread_out(ref, axis, here, size, rows=slice(None)):
        return [
            send(ref.at[0, rows], ref.at[d, rows], {axis: peer(here, d, size)})
            for d in range(1, size)
        ]

    def receive(copies):
        for copy in copies:
            copy.wait_recv()

    late = []

    def share_perturb(part):
        here = slice(p.members * part // ITERS, p.members * (part + 1) // ITERS)
        for d in range(1, p.mems if p.share and here.stop > here.start else 1):
            target = {"mem": peer(at_mem, d, p.mems)}
            late.append(send(perturb_in.at[here], others.at[d - 1, here], target))

    share_perturb(0)

    loads[0].wait()
    row, column = split_cell(cell[...], p.fine_lon)
    row_weight[...] = interpolation(row, p.pad_lat).astype(jnp.bfloat16)
    column_weight[...] = interpolation(column, p.pad_lon)
    loads[1].wait()
    for start in range(0, p.slots, p.chunk):
        here = slice(start, start + p.chunk)
        chosen = lax.broadcasted_iota(jnp.int32, (p.fine_lon, p.chunk), 0) == column[:, here]
        chosen = chosen.astype(jnp.float32).astype(jnp.bfloat16)
        wanted = lax.broadcasted_iota(jnp.int32, (p.fine_lat, p.chunk), 0) == row[:, here]
        for k in range(p.members):
            picked = product(split(perturb[k]), chosen, NN)
            at_obs[k : k + 1, here] = p.scale * jnp.sum(
                jnp.where(wanted, picked, 0.0), axis=0, keepdims=True
            )

    own_rows = p.pad_lon

    def form_lon_factors():
        lon_ext = kernel_rows(
            lon_scales[...], *extended_index(p.lons, p.pad_lon, p.tile_lon, at_lon, p.total_lon)
        )
        lon_ext = split(lon_ext)
        lon_own = tuple(term[:own_rows] for term in lon_ext)
        put(lon_factor.at[:, :own_rows], product(lon_own, lon_ext, NT))
        picks = select_rows(p.tile_lon, at_lon * p.tile_lon, p.total_lon).astype(jnp.bfloat16)
        put(lon_factor.at[:, own_rows:], product(picks, lon_ext, NT))

    def form_lat_factors():
        lat_ext = kernel_rows(
            lat_scales[...], *extended_index(p.lats, p.pad_lat, p.tile_lat, at_lat, p.total_lat)
        )
        lat_ext = split(lat_ext)
        lat_own = tuple(term[: p.pad_lat] for term in lat_ext)
        put(lat_factor, product(lat_ext, lat_own, NT))
        picks = select_rows(p.tile_lat, at_lat * p.tile_lat, p.total_lat).astype(jnp.bfloat16)
        put(lat_grad, product(picks, lat_ext, NT))
        to_rows[...] = interpolation(
            lax.broadcasted_iota(jnp.int32, (1, p.fine_lat), 1), p.pad_lat
        ).astype(jnp.bfloat16)
        to_columns[...] = interpolation(
            lax.broadcasted_iota(jnp.int32, (1, p.fine_lon), 1), p.pad_lon
        ).astype(jnp.bfloat16)

    for load in loads[2:]:
        load.wait()
    usable = lax.broadcasted_iota(jnp.int32, (1, p.slots), 1) < count[...]
    usable = usable.astype(jnp.float32)
    inverse = 1.0 / error[...]
    observed = jnp.zeros((1, p.slots), jnp.float32)
    dual = jnp.zeros((1, p.slots), jnp.float32)
    lengths, grad_copies, coarse_copies = [], [], []
    for it in range(ITERS):
        residual = (observed - innov[...]) * inverse
        bounded = residual * lax.rsqrt(1.0 + (residual / huber_width) ** 2)
        step = dual + usable * bounded * inverse
        term, strip, grad = terms.at[it], strips.at[it], grads.at[it]
        spans = [slice(k * p.pad_lon, (k + 1) * p.pad_lon) for k in range(p.members)]
        term_copies, strip_copies, pieces = [], [], []
        for k in range(p.members):
            weighted = split(column_weight[...] * (step * at_obs[k : k + 1, :]))
            term[0, spans[k]] = product(weighted, row_weight[...], NT)
            term_copies.append(spread_out(term, "lon", at_lon, p.lons, spans[k]))
        if it == 0:
            form_lon_factors()
        for k in range(p.members):
            receive(term_copies[k])
            pieces.append(split(jnp.concatenate([term[d, spans[k]] for d in range(p.lons)])))
            near = (lon_factor[0, :own_rows], lon_factor[1, :own_rows])
            strip[0, spans[k]] = product(near, pieces[k], NN)
            strip_copies.append(spread_out(strip, "lat", at_lat, p.lats, spans[k]))
        for k in range(p.members):
            near = (lon_factor[0, own_rows:], lon_factor[1, own_rows:])
            grad[0, k * p.tile_lon : (k + 1) * p.tile_lon] = product(near, pieces[k], NN)
        if it == 0:
            form_lat_factors()
        image = jnp.zeros((1, p.slots), jnp.float32)
        for k in range(p.members):
            receive(strip_copies[k])
            coarse = None
            for d in range(p.lats):
                there = slice(d * p.pad_lat, (d + 1) * p.pad_lat)
                near = (lat_factor[0, there], lat_factor[1, there])
                part = product(split(strip[d, spans[k]]), near, NN)
                coarse = part if coarse is None else coarse + part
            coarses[it, 0, spans[k]] = coarse
            rows = product(split(coarse), row_weight[...], NN)
            image = image + at_obs[k : k + 1, :] * jnp.sum(
                rows * column_weight[...], axis=0, keepdims=True
            )
        images[it, 0] = image
        image_copies = spread_out(images.at[it], "mem", at_mem, p.mems)
        if p.share:
            late += spread_out(coarses.at[it], "mem", at_mem, p.mems)
        late += spread_out(grad, "lat", at_lat, p.lats)
        receive(image_copies)
        for d in range(1, p.mems):
            image = image + images[it, d]
        grad_part = jnp.sum(step * image, axis=1, keepdims=True)
        curve_part = jnp.sum(usable * (image * inverse) ** 2, axis=1, keepdims=True)
        first = lax.broadcasted_iota(jnp.int32, (8, 128), 0) == 0
        sums[it, 0] = jnp.where(first, grad_part, curve_part)
        receive(
            [
                send(sums.at[it, 0], sums.at[it, a * p.lons + b], in_group(a, b))
                for a, b in group
            ]
        )
        total = jnp.sum(sums[it], axis=0)
        grad_total, curvature = total[0:1, 0:1], total[1:2, 0:1]
        length = grad_total / (grad_total + curvature + tiny_floor)
        lengths.append(length)
        observed = observed - length * image
        dual = dual - length * step
        if it + 1 < ITERS:
            share_perturb(it + 1)
    receive(late)

    def combined(ref, place):
        return -sum(lengths[it] * ref[(it,) + place] for it in range(ITERS))

    for k in range(p.members):
        own = None
        for d in range(p.lats):
            there = slice(d * p.pad_lat, (d + 1) * p.pad_lat)
            strip = split(combined(grads, (d, slice(k * p.tile_lon, (k + 1) * p.tile_lon))))
            part = product((lat_grad[0, :, there], lat_grad[1, :, there]), strip, NT)
            own = part if own is None else own + part
        analysis[k] = own
    field = None
    for d in range(p.mems if p.share else 1):
        partial = None
        for k in range(p.members):
            coarse = combined(coarses, (d, slice(k * p.pad_lon, (k + 1) * p.pad_lon)))
            wide = lax.dot_general(
                to_rows[...],
                split(coarse)[0],
                (((0,), (1,)), ((), ())),
                preferred_element_type=jnp.float32,
            ) + lax.dot_general(
                to_rows[...],
                split(coarse)[1],
                (((0,), (1,)), ((), ())),
                preferred_element_type=jnp.float32,
            )
            fine = product(split(wide), to_columns[...], NN)
            here = perturb[k] if d == 0 else others[d - 1, k]
            partial = fine * here if partial is None else partial + fine * here
        field = partial if field is None else field + partial
    increment[...] = p.scale * field
    for copy in started:
        copy.wait_send()


def per_device(perturb, loc_lat, loc_lon, obs_cell, obs_count, obs_innov, obs_error):
    p = Plan(
        perturb.shape,
        obs_cell.shape[-1],
        loc_lat.shape[0],
        loc_lon.shape[0],
        tuple(lax.axis_size(name) for name in ("mem", "lat", "lon")),
    )
    f32, bf16 = jnp.float32, jnp.bfloat16
    coarse_rows = p.members * p.pad_lon
    grad_rows = p.members * p.tile_lon
    in_vmem = pl.BlockSpec(memory_space=pltpu.VMEM)
    groups = p.mems if p.share else 1
    analysis, increment = pl.pallas_call(
        lambda *refs: body(p, *refs),
        out_shape=(
            jax.ShapeDtypeStruct((p.members, p.tile_lat, p.tile_lon), f32),
            jax.ShapeDtypeStruct((p.fine_lat, p.fine_lon), f32),
        ),
        in_specs=[pl.BlockSpec(memory_space=pl.ANY)] * 7,
        out_specs=(in_vmem, in_vmem),
        scratch_shapes=[
            pltpu.VMEM(perturb.shape, f32),
            pltpu.VMEM((1, p.total_lat), f32),
            pltpu.VMEM((1, p.total_lon), f32),
            pltpu.VMEM((1, p.slots), jnp.int32),
            pltpu.VMEM((1, 1), jnp.int32),
            pltpu.VMEM((1, p.slots), f32),
            pltpu.VMEM((1, p.slots), f32),
            pltpu.SemaphoreType.DMA((7,)),
            pltpu.VMEM((max(groups - 1, 1),) + perturb.shape, f32),
            pltpu.VMEM((p.pad_lon, p.slots), f32),
            pltpu.VMEM((p.pad_lat, p.slots), bf16),
            pltpu.VMEM((p.members, p.slots), f32),
            pltpu.VMEM((2, p.pad_lon + p.tile_lon, p.lons * p.pad_lon), bf16),
            pltpu.VMEM((2, p.lats * p.pad_lat, p.pad_lat), bf16),
            pltpu.VMEM((2, p.tile_lat, p.lats * p.pad_lat), bf16),
            pltpu.VMEM((p.pad_lat, p.fine_lat), bf16),
            pltpu.VMEM((p.pad_lon, p.fine_lon), bf16),
            pltpu.VMEM((ITERS, p.lons, coarse_rows, p.pad_lat), f32),
            pltpu.VMEM((ITERS, p.lats, coarse_rows, p.pad_lat), f32),
            pltpu.VMEM((ITERS, p.lats, grad_rows, p.pad_lat), f32),
            pltpu.VMEM((ITERS, groups, coarse_rows, p.pad_lat), f32),
            pltpu.VMEM((ITERS, p.mems, 1, p.slots), f32),
            pltpu.VMEM((ITERS, p.lats * p.lons, 8, 128), f32),
            pltpu.SemaphoreType.DMA((p.copies,)),
            pltpu.SemaphoreType.DMA((p.copies,)),
        ],
        compiler_params=pltpu.CompilerParams(
            collective_id=0, has_side_effects=True, vmem_limit_bytes=60 << 20
        ),
    )(
        perturb,
        loc_lat.reshape(1, -1),
        loc_lon.reshape(1, -1),
        obs_cell.reshape(1, -1),
        obs_count,
        obs_innov.reshape(1, -1),
        obs_error.reshape(1, -1),
    )
    if not p.share:
        increment = lax.psum(increment, "mem")
    return analysis, increment


def solution(mesh):
    placed = (
        P("mem", "lat", "lon"),
        P(),
        P(),
        P("lat", "lon", None),
        P("lat", "lon"),
        P("lat", "lon", None),
        P("lat", "lon", None),
    )
    return jax.shard_map(
        per_device,
        mesh=mesh,
        in_specs=placed,
        out_specs=(P("mem", "lat", "lon"), P("lat", "lon")),
        check_vma=False,
    )
```

```python
import math

import jax
import jax.numpy as jnp
from jax import lax
from jax.experimental import pallas as pl
from jax.experimental.pallas import tpu as pltpu
from jax.sharding import PartitionSpec as P

ITERS = 2
huber_width = 1.0
tiny_floor = 1e-06

NN = (((1,), (0,)), ((), ()))
NT = (((1,), (1,)), ((), ()))


def round_up(count, unit):
    return -(-count // unit) * unit


def extended_index(tiles, pad, tile, first, total):
    row = lax.broadcasted_iota(jnp.int32, (tiles * pad, 1), 0)
    at = jnp.zeros_like(row)
    for later in range(1, tiles):
        at = at + (row >= later * pad).astype(jnp.int32)
    inner = row - at * pad
    which = first - at
    which = jnp.where(which < 0, which + tiles, which)
    index = which * tile - 1 + inner
    valid = (inner < tile + 2) & (index >= 0) & (index < total)
    return index, valid


def kernel_rows(scales, index, valid):
    column = lax.broadcasted_iota(jnp.int32, (index.shape[0], scales.shape[1]), 1)
    row_scale = jnp.sum(jnp.where(column == index, scales, 0.0), axis=1, keepdims=True)
    row_scale = jnp.where(valid, row_scale, 1.0)
    offset = (index - column).astype(jnp.float32)
    weight = jnp.where(valid, lax.rsqrt(math.sqrt(math.pi) * row_scale), 0.0)
    return weight * jnp.exp(-(offset * offset) / (row_scale * row_scale + scales * scales))


def select_rows(count, first, total):
    row = lax.broadcasted_iota(jnp.int32, (count, total), 0) + first
    column = lax.broadcasted_iota(jnp.int32, (count, total), 1)
    return (row == column).astype(jnp.float32)


def interpolation(fine, pad):
    below = fine >> 2
    phase = (fine & 3).astype(jnp.float32)
    lower = jnp.maximum(0.375 - 0.25 * phase, 0.0)
    upper = jnp.maximum(0.25 * phase - 0.375, 0.0)
    middle = 1.0 - lower - upper
    cell = lax.broadcasted_iota(jnp.int32, (pad, fine.shape[1]), 0) - below
    return jnp.where(
        cell == 0,
        lower,
        jnp.where(cell == 1, middle, jnp.where(cell == 2, upper, 0.0)),
    )


def split_cell(cell, width):
    if width & (width - 1) == 0:
        row = cell >> (width.bit_length() - 1)
    else:
        row = lax.div(cell, jnp.int32(width))
    return row, cell - row * width


def split(values):
    high = values.astype(jnp.bfloat16)
    return high, (values - high.astype(jnp.float32)).astype(jnp.bfloat16)


def multiply(left, right, dims):
    return lax.dot_general(left, right, dims, preferred_element_type=jnp.float32)


def product(left, right, dims):
    if not isinstance(left, tuple):
        return multiply(left, right[0], dims) + multiply(left, right[1], dims)
    if not isinstance(right, tuple):
        return multiply(left[0], right, dims) + multiply(left[1], right, dims)
    return (
        multiply(left[0], right[0], dims)
        + multiply(left[0], right[1], dims)
        + multiply(left[1], right[0], dims)
    )


def put(ref, values):
    high, low = split(values)
    ref[0] = high
    ref[1] = low


class Plan:
    def __init__(self, perturb, slots, total_lat, total_lon, axes):
        self.members, self.fine_lat, self.fine_lon = perturb
        self.tile_lat, self.tile_lon = self.fine_lat // 4, self.fine_lon // 4
        self.slots, self.total_lat, self.total_lon = slots, total_lat, total_lon
        self.mems, self.lats, self.lons = axes
        self.pad_lat = round_up(self.tile_lat + 2, 128)
        self.pad_lon = round_up(self.tile_lon + 2, 16)
        self.scale = 1.0 / math.sqrt(self.members * self.mems - 1)
        self.chunk = math.gcd(slots, 512)
        self.share = self.mems * math.prod(perturb) <= 1 << 21
        group = self.lats * self.lons
        self.copies = ITERS * (self.mems - 1) + ITERS * (
            self.members * (self.lons - 1)
            + self.members * (self.lats - 1)
            + self.lats - 1
            + 2 * (self.mems - 1)
            + group - 1
        )


def body(
    plan,
    perturb_in,
    lat_scales_in,
    lon_scales_in,
    cell_in,
    count_in,
    innov_in,
    error_in,
    analysis,
    increment,
    perturb,
    lat_scales,
    lon_scales,
    cell,
    count,
    innov,
    error,
    load_sem,
    others,
    column_weight,
    row_weight,
    at_obs,
    lon_factor,
    lat_factor,
    lat_grad,
    to_rows,
    to_columns,
    terms,
    strips,
    grads,
    coarses,
    images,
    sums,
    send_sem,
    recv_sem,
):
    p = plan
    loads = []
    for at, (source, target) in enumerate(
        [
            (cell_in, cell),
            (perturb_in, perturb),
            (count_in, count),
            (innov_in, innov),
            (error_in, error),
            (lon_scales_in, lon_scales),
            (lat_scales_in, lat_scales),
        ]
    ):
        loads.append(pltpu.make_async_copy(source, target, load_sem.at[at]))
        loads[-1].start()
    at_mem, at_lat, at_lon = (lax.axis_index(name) for name in ("mem", "lat", "lon"))

    def peer(here, distance, size):
        return lax.rem(here + distance, size)

    group = [(a, b) for a in range(p.lats) for b in range(p.lons) if a or b]

    def in_group(a, b):
        return {"lat": peer(at_lat, a, p.lats), "lon": peer(at_lon, b, p.lons)}

    barrier = pltpu.get_barrier_semaphore()
    for a, b in group:
        pl.semaphore_signal(
            barrier, inc=1, device_id=in_group(a, b), device_id_type=pl.DeviceIdType.MESH
        )
    for d in range(1, p.mems):
        pl.semaphore_signal(
            barrier,
            inc=1,
            device_id={"mem": peer(at_mem, d, p.mems)},
            device_id_type=pl.DeviceIdType.MESH,
        )
    pl.semaphore_wait(barrier, len(group) + p.mems - 1)

    started = []

    def send(source, target, device):
        at = len(started)
        copy = pltpu.make_async_remote_copy(
            src_ref=source,
            dst_ref=target,
            send_sem=send_sem.at[at],
            recv_sem=recv_sem.at[at],
            device_id=device,
            device_id_type=pl.DeviceIdType.MESH,
        )
        copy.start()
        started.append(copy)
        return copy

    def spread_out(ref, axis, here, size, rows=slice(None)):
        return [
            send(ref.at[0, rows], ref.at[d, rows], {axis: peer(here, d, size)})
            for d in range(1, size)
        ]

    def receive(copies):
        for copy in copies:
            copy.wait_recv()

    late = []

    def share_perturb(part):
        here = slice(p.members * part // ITERS, p.members * (part + 1) // ITERS)
        for d in range(1, p.mems if p.share and here.stop > here.start else 1):
            target = {"mem": peer(at_mem, d, p.mems)}
            late.append(send(perturb_in.at[here], others.at[d - 1, here], target))

    share_perturb(0)

    loads[0].wait()
    row, column = split_cell(cell[...], p.fine_lon)
    row_weight[...] = interpolation(row, p.pad_lat).astype(jnp.bfloat16)
    column_weight[...] = interpolation(column, p.pad_lon)
    loads[1].wait()
    for start in range(0, p.slots, p.chunk):
        here = slice(start, start + p.chunk)
        chosen = lax.broadcasted_iota(jnp.int32, (p.fine_lon, p.chunk), 0) == column[:, here]
        chosen = chosen.astype(jnp.float32).astype(jnp.bfloat16)
        wanted = lax.broadcasted_iota(jnp.int32, (p.fine_lat, p.chunk), 0) == row[:, here]
        for k in range(p.members):
            picked = product(split(perturb[k]), chosen, NN)
            at_obs[k : k + 1, here] = p.scale * jnp.sum(
                jnp.where(wanted, picked, 0.0), axis=0, keepdims=True
            )

    own_rows = p.pad_lon

    def form_lon_factors():
        lon_ext = kernel_rows(
            lon_scales[...], *extended_index(p.lons, p.pad_lon, p.tile_lon, at_lon, p.total_lon)
        )
        lon_ext = split(lon_ext)
        lon_own = tuple(term[:own_rows] for term in lon_ext)
        put(lon_factor.at[:, :own_rows], product(lon_own, lon_ext, NT))
        picks = select_rows(p.tile_lon, at_lon * p.tile_lon, p.total_lon).astype(jnp.bfloat16)
        put(lon_factor.at[:, own_rows:], product(picks, lon_ext, NT))

    def form_lat_factors():
        lat_ext = kernel_rows(
            lat_scales[...], *extended_index(p.lats, p.pad_lat, p.tile_lat, at_lat, p.total_lat)
        )
        lat_ext = split(lat_ext)
        lat_own = tuple(term[: p.pad_lat] for term in lat_ext)
        put(lat_factor, product(lat_ext, lat_own, NT))
        picks = select_rows(p.tile_lat, at_lat * p.tile_lat, p.total_lat).astype(jnp.bfloat16)
        put(lat_grad, product(picks, lat_ext, NT))
        to_rows[...] = interpolation(
            lax.broadcasted_iota(jnp.int32, (1, p.fine_lat), 1), p.pad_lat
        ).astype(jnp.bfloat16)
        to_columns[...] = interpolation(
            lax.broadcasted_iota(jnp.int32, (1, p.fine_lon), 1), p.pad_lon
        ).astype(jnp.bfloat16)

    for load in loads[2:]:
        load.wait()
    usable = lax.broadcasted_iota(jnp.int32, (1, p.slots), 1) < count[...]
    usable = usable.astype(jnp.float32)
    inverse = 1.0 / error[...]
    observed = jnp.zeros((1, p.slots), jnp.float32)
    dual = jnp.zeros((1, p.slots), jnp.float32)
    lengths, grad_copies, coarse_copies = [], [], []
    for it in range(ITERS):
        residual = (observed - innov[...]) * inverse
        bounded = residual * lax.rsqrt(1.0 + (residual / huber_width) ** 2)
        step = dual + usable * bounded * inverse
        term, strip, grad = terms.at[it], strips.at[it], grads.at[it]
        spans = [slice(k * p.pad_lon, (k + 1) * p.pad_lon) for k in range(p.members)]
        term_copies, strip_copies, pieces = [], [], []
        for k in range(p.members):
            weighted = split(column_weight[...] * (step * at_obs[k : k + 1, :]))
            term[0, spans[k]] = product(weighted, row_weight[...], NT)
            term_copies.append(spread_out(term, "lon", at_lon, p.lons, spans[k]))
        if it == 0:
            form_lon_factors()
        for k in range(p.members):
            receive(term_copies[k])
            pieces.append(split(jnp.concatenate([term[d, spans[k]] for d in range(p.lons)])))
            near = (lon_factor[0, :own_rows], lon_factor[1, :own_rows])
            strip[0, spans[k]] = product(near, pieces[k], NN)
            strip_copies.append(spread_out(strip, "lat", at_lat, p.lats, spans[k]))
        for k in range(p.members):
            near = (lon_factor[0, own_rows:], lon_factor[1, own_rows:])
            grad[0, k * p.tile_lon : (k + 1) * p.tile_lon] = product(near, pieces[k], NN)
        if it == 0:
            form_lat_factors()
        image = jnp.zeros((1, p.slots), jnp.float32)
        for k in range(p.members):
            receive(strip_copies[k])
            coarse = None
            for d in range(p.lats):
                there = slice(d * p.pad_lat, (d + 1) * p.pad_lat)
                near = (lat_factor[0, there], lat_factor[1, there])
                part = product(split(strip[d, spans[k]]), near, NN)
                coarse = part if coarse is None else coarse + part
            coarses[it, 0, spans[k]] = coarse
            rows = product(split(coarse), row_weight[...], NN)
            image = image + at_obs[k : k + 1, :] * jnp.sum(
                rows * column_weight[...], axis=0, keepdims=True
            )
        images[it, 0] = image
        image_copies = spread_out(images.at[it], "mem", at_mem, p.mems)
        receive(image_copies)
        for d in range(1, p.mems):
            image = image + images[it, d]
        grad_part = jnp.sum(step * image, axis=1, keepdims=True)
        curve_part = jnp.sum(usable * (image * inverse) ** 2, axis=1, keepdims=True)
        first = lax.broadcasted_iota(jnp.int32, (8, 128), 0) == 0
        sums[it, 0] = jnp.where(first, grad_part, curve_part)
        sum_copies = [
            send(sums.at[it, 0], sums.at[it, a * p.lons + b], in_group(a, b)) for a, b in group
        ]
        if p.share:
            late += spread_out(coarses.at[it], "mem", at_mem, p.mems)
        late += spread_out(grad, "lat", at_lat, p.lats)
        receive(sum_copies)
        total = jnp.sum(sums[it], axis=0)
        grad_total, curvature = total[0:1, 0:1], total[1:2, 0:1]
        length = grad_total / (grad_total + curvature + tiny_floor)
        lengths.append(length)
        observed = observed - length * image
        dual = dual - length * step
        if it + 1 < ITERS:
            share_perturb(it + 1)
    receive(late)

    def combined(ref, place):
        return -sum(lengths[it] * ref[(it,) + place] for it in range(ITERS))

    for k in range(p.members):
        own = None
        for d in range(p.lats):
            there = slice(d * p.pad_lat, (d + 1) * p.pad_lat)
            strip = split(combined(grads, (d, slice(k * p.tile_lon, (k + 1) * p.tile_lon))))
            part = product((lat_grad[0, :, there], lat_grad[1, :, there]), strip, NT)
            own = part if own is None else own + part
        analysis[k] = own
    field = None
    for d in range(p.mems if p.share else 1):
        partial = None
        for k in range(p.members):
            coarse = combined(coarses, (d, slice(k * p.pad_lon, (k + 1) * p.pad_lon)))
            wide = lax.dot_general(
                to_rows[...],
                split(coarse)[0],
                (((0,), (1,)), ((), ())),
                preferred_element_type=jnp.float32,
            ) + lax.dot_general(
                to_rows[...],
                split(coarse)[1],
                (((0,), (1,)), ((), ())),
                preferred_element_type=jnp.float32,
            )
            fine = product(split(wide), to_columns[...], NN)
            here = perturb[k] if d == 0 else others[d - 1, k]
            partial = fine * here if partial is None else partial + fine * here
        field = partial if field is None else field + partial
    increment[...] = p.scale * field
    for copy in started:
        copy.wait_send()


def per_device(perturb, loc_lat, loc_lon, obs_cell, obs_count, obs_innov, obs_error):
    p = Plan(
        perturb.shape,
        obs_cell.shape[-1],
        loc_lat.shape[0],
        loc_lon.shape[0],
        tuple(lax.axis_size(name) for name in ("mem", "lat", "lon")),
    )
    f32, bf16 = jnp.float32, jnp.bfloat16
    coarse_rows = p.members * p.pad_lon
    grad_rows = p.members * p.tile_lon
    in_vmem = pl.BlockSpec(memory_space=pltpu.VMEM)
    groups = p.mems if p.share else 1
    analysis, increment = pl.pallas_call(
        lambda *refs: body(p, *refs),
        out_shape=(
            jax.ShapeDtypeStruct((p.members, p.tile_lat, p.tile_lon), f32),
            jax.ShapeDtypeStruct((p.fine_lat, p.fine_lon), f32),
        ),
        in_specs=[pl.BlockSpec(memory_space=pl.ANY)] * 7,
        out_specs=(in_vmem, in_vmem),
        scratch_shapes=[
            pltpu.VMEM(perturb.shape, f32),
            pltpu.VMEM((1, p.total_lat), f32),
            pltpu.VMEM((1, p.total_lon), f32),
            pltpu.VMEM((1, p.slots), jnp.int32),
            pltpu.VMEM((1, 1), jnp.int32),
            pltpu.VMEM((1, p.slots), f32),
            pltpu.VMEM((1, p.slots), f32),
            pltpu.SemaphoreType.DMA((7,)),
            pltpu.VMEM((max(groups - 1, 1),) + perturb.shape, f32),
            pltpu.VMEM((p.pad_lon, p.slots), f32),
            pltpu.VMEM((p.pad_lat, p.slots), bf16),
            pltpu.VMEM((p.members, p.slots), f32),
            pltpu.VMEM((2, p.pad_lon + p.tile_lon, p.lons * p.pad_lon), bf16),
            pltpu.VMEM((2, p.lats * p.pad_lat, p.pad_lat), bf16),
            pltpu.VMEM((2, p.tile_lat, p.lats * p.pad_lat), bf16),
            pltpu.VMEM((p.pad_lat, p.fine_lat), bf16),
            pltpu.VMEM((p.pad_lon, p.fine_lon), bf16),
            pltpu.VMEM((ITERS, p.lons, coarse_rows, p.pad_lat), f32),
            pltpu.VMEM((ITERS, p.lats, coarse_rows, p.pad_lat), f32),
            pltpu.VMEM((ITERS, p.lats, grad_rows, p.pad_lat), f32),
            pltpu.VMEM((ITERS, groups, coarse_rows, p.pad_lat), f32),
            pltpu.VMEM((ITERS, p.mems, 1, p.slots), f32),
            pltpu.VMEM((ITERS, p.lats * p.lons, 8, 128), f32),
            pltpu.SemaphoreType.DMA((p.copies,)),
            pltpu.SemaphoreType.DMA((p.copies,)),
        ],
        compiler_params=pltpu.CompilerParams(
            collective_id=0, has_side_effects=True, vmem_limit_bytes=60 << 20
        ),
    )(
        perturb,
        loc_lat.reshape(1, -1),
        loc_lon.reshape(1, -1),
        obs_cell.reshape(1, -1),
        obs_count,
        obs_innov.reshape(1, -1),
        obs_error.reshape(1, -1),
    )
    if not p.share:
        increment = lax.psum(increment, "mem")
    return analysis, increment


def solution(mesh):
    placed = (
        P("mem", "lat", "lon"),
        P(),
        P(),
        P("lat", "lon", None),
        P("lat", "lon"),
        P("lat", "lon", None),
        P("lat", "lon", None),
    )
    return jax.shard_map(
        per_device,
        mesh=mesh,
        in_specs=placed,
        out_specs=(P("mem", "lat", "lon"), P("lat", "lon")),
        check_vma=False,
    )
```
